32 devices in a mesh: grp: 2 (over x), blk: 16 (over z, y, core).
Axes of the slice: x: 2, y: 2, z: 4, core: 2. Of those that a mesh axis runs over, the one named last changes fastest.
Arguments:
- sim_embed: bfloat16 [4096, 512], P(('grp', 'blk')), parts along dimension 0, may hold values from -6 to 6
- real_embed: bfloat16 [2816, 512], P(('grp', 'blk')), parts along dimension 0, may hold values from -4.5 to 4.5
Outputs:
- sim_grad: float32 [4096, 512], P(('grp', 'blk')), parts along dimension 0
The draws below stay inside these ranges and needn't reach their ends.
There are 2 independent parts, one for each index of `grp`. The reference program is written for one: setup_inputs(seed, part) draws one part's arguments, and reference() takes and returns one part's arrays. A program takes and returns all parts, laid end to end along the dimension named above; each array names one. Nothing has to cross between parts.
All inputs are finite; a program needn't handle non-finite values.
Results may differ from the reference program's by a relative error of at most 0.00075.
Values may be sent and summed in bfloat16 or wider, within the bound.
A program may use at most 64 MiB of HBM per device.

```python
import jax
import jax.numpy as jnp
from jax import lax

D = 512
SIM_DEV = 128
SIMS = 2048
REALS = 1408


def shared_parts(key):
    centers = jax.random.normal(jax.random.fold_in(key, 101), (8, D), jnp.float32)
    return centers


def draw_sim_embed(key, part):
    centers = shared_parts(key)
    key = jax.random.fold_in(key, 3)
    assign = jax.random.randint(jax.random.fold_in(key, 1), (SIMS,), 0, 8)
    picked = jnp.take(centers, assign, axis=0)
    noise = 0.5 * jax.random.normal(jax.random.fold_in(key, 2), (SIMS, D), jnp.float32)
    values = 1.2 * picked + noise
    return jnp.clip(values, -6.0, 6.0).astype(jnp.bfloat16)


def draw_real_embed(key, part):
    centers = shared_parts(key)
    key = jax.random.fold_in(key, 7)
    assign = jax.random.randint(jax.random.fold_in(key, 1), (REALS,), 0, 8)
    picked = jnp.take(centers, assign, axis=0)
    noise = 0.5 * jax.random.normal(jax.random.fold_in(key, 2), (REALS, D), jnp.float32)
    values = 0.96 * picked + noise
    return jnp.clip(values, -4.5, 4.5).astype(jnp.bfloat16)


def setup_inputs(seed: int = 0, part: int = 0) -> dict:
    keys = jax.random.split(jax.random.key(seed), 3)
    own_keys = jax.random.split(jax.random.fold_in(keys[2], part), 3)
    return {
        "sim_embed": draw_sim_embed(jax.random.fold_in(jax.random.fold_in(keys[2], part), 71), part),
        "real_embed": draw_real_embed(jax.random.fold_in(jax.random.fold_in(keys[2], part), 71), part),
    }


SCALES = (0.125, 0.25, 0.5, 1.0, 2.0)


def kernel_weights(distance, width):
    total = jnp.zeros(distance.shape, jnp.float32)
    for factor in SCALES:
        total = total + factor * jnp.exp(-factor * distance / width)
    return total


def squares(block):
    values = block.astype(jnp.float32)
    return jnp.sum(values * values, axis=1)


def pair_weights(left, left_norm, right, right_norm, width):
    gram = lax.dot_general(left, right, (((1,), (1,)), ((), ())), preferred_element_type=jnp.float32)
    return kernel_weights(left_norm[:, None] + right_norm[None, :] - 2.0 * gram, width)


def reference(sim_embed, real_embed):
    count_sim = sim_embed.shape[0]
    count_real = real_embed.shape[0]
    width = sim_embed.shape[1]
    norms_sim = squares(sim_embed)
    norms_real = squares(real_embed)
    rows = 4 * SIM_DEV
    blocks = sim_embed.reshape(count_sim // rows, rows, width)
    block_norms = norms_sim.reshape(count_sim // rows, rows)

    def one_block(pieces):
        rows_x, rows_norm = pieces
        rows_f = rows_x.astype(jnp.float32)
        weight_xx = pair_weights(rows_x, rows_norm, sim_embed, norms_sim, width)
        weight_xx_b = weight_xx.astype(jnp.bfloat16)
        near_xx = rows_f * jnp.sum(weight_xx, axis=1)[:, None] - jnp.dot(weight_xx_b, sim_embed, preferred_element_type=jnp.float32)
        weight_xy = pair_weights(rows_x, rows_norm, real_embed, norms_real, width)
        weight_xy_b = weight_xy.astype(jnp.bfloat16)
        near_xy = rows_f * jnp.sum(weight_xy, axis=1)[:, None] - jnp.dot(weight_xy_b, real_embed, preferred_element_type=jnp.float32)
        return near_xy / count_real - near_xx / count_sim

    result = lax.map(one_block, (blocks, block_norms))
    return result.reshape(count_sim, width)
```

```python
import functools
import math

import jax
import jax.numpy as jnp
from jax import lax
from jax.experimental import pallas as pl
from jax.experimental.pallas import tpu as pltpu
from jax.sharding import PartitionSpec as P

MESH = pl.DeviceIdType.MESH
CORES = 2
RIGHTWARD, LEFTWARD = 0, 1
SIM, REAL = 0, 1


def grid_sides(chips):
    inner = max(k for k in range(2, chips + 1, 2) if k * k <= chips and chips % k == 0)
    return chips // inner, inner


def place_on_cycle(chip, outer, inner):
    z, y = chip // inner, chip % inner
    run = outer - 1
    down = (z - 1) + (y % 2) * (outer - 2 * z)
    back = 1 + inner * run + (inner - 1 - y)
    return jnp.where(z > 0, 1 + y * run + down, jnp.where(y == 0, 0, back))


def chip_on_cycle(place, outer, inner):
    run = outer - 1
    q = jnp.maximum(place - 1, 0)
    y, r = q // run, q % run
    z = 1 + r + (y % 2) * (outer - 2 - 2 * r)
    back = inner - 1 - (q - inner * run)
    inside = z * inner + y
    return jnp.where(place == 0, 0, jnp.where(q < inner * run, inside, back))


def kernel(
    chips, count_sim, count_real,
    sim_ref, real_ref, out_ref,
    sims, reals, query, total, partial, arrived,
    send_sem, recv_sem, near_send, near_recv,
):
    half = chips // 2
    outer, inner = grid_sides(chips)
    rows, width = sim_ref.shape
    me = lax.axis_index("blk")
    core = me % CORES
    place = place_on_cycle(me // CORES, outer, inner)
    right = chip_on_cycle((place + 1) % chips, outer, inner) * CORES + core
    left = chip_on_cycle((place + chips - 1) % chips, outer, inner) * CORES + core
    sibling = me + 1 - 2 * core

    barrier = pltpu.get_barrier_semaphore()
    for other in (left, right, sibling):
        pl.semaphore_signal(barrier, inc=1, device_id={"blk": other}, device_id_type=MESH)
    pl.semaphore_wait(barrier, 3)

    def ring_copy(way, kind, distance):
        own, slots = ((sim_ref, sims), (real_ref, reals))[kind]
        source = own if isinstance(distance, int) and distance == 1 else slots.at[distance - 2, way]
        return pltpu.make_async_remote_copy(
            src_ref=source,
            dst_ref=slots.at[distance - 1, way],
            send_sem=send_sem.at[way, kind, distance - 1],
            recv_sem=recv_sem.at[way, kind, distance - 1],
            device_id={"blk": right if way == RIGHTWARD else left},
            device_id_type=MESH,
        )

    own_rows = pltpu.make_async_remote_copy(
        src_ref=sim_ref, dst_ref=query.at[1], send_sem=near_send.at[0], recv_sem=near_recv.at[0],
        device_id={"blk": sibling}, device_id_type=MESH,
    )
    own_rows.start()
    for kind in (SIM, REAL):
        for way in (RIGHTWARD, LEFTWARD):
            ring_copy(way, kind, 1).start()

    query[0] = sim_ref[...]
    rate = 0.125 / width * math.log2(math.e)

    def row_norms(block):
        values = block.astype(jnp.float32)
        return jnp.sum(values * values, axis=1, keepdims=True) * rate

    def across(column):
        return jnp.transpose(jnp.broadcast_to(column, (column.shape[0], 128)))[0:1]

    def pull(rows_b, rows_norm, keys, scale):
        gram = lax.dot_general(
            rows_b, keys, (((1,), (1,)), ((), ())), preferred_element_type=jnp.float32
        )
        e1 = jnp.exp2((2.0 * rate) * gram - (rows_norm + across(row_norms(keys))))
        e2 = e1 * e1
        e4 = e2 * e2
        e8 = e4 * e4
        weight = 0.125 * e1 + 0.25 * e2 + 0.5 * e4 + e8 + 2.0 * (e8 * e8)
        pulled = jnp.dot(weight.astype(jnp.bfloat16), keys, preferred_element_type=jnp.float32)
        return jnp.sum(weight, axis=1, keepdims=True) * scale, pulled * scale

    own_rows.wait_recv()
    everyone = query[...].reshape(CORES * rows, width)
    every_norm = row_norms(everyone)

    def weigh(blocks, scale, sums):
        for keys in blocks:
            summed, pulled = pull(everyone, every_norm, keys, scale)
            total[...] -= pulled
            sums = sums + summed
        return sums

    per_sim, per_real = -1.0 / count_sim, 1.0 / count_real
    total[...] = jnp.zeros_like(total)
    sums = jnp.zeros((CORES * rows, 1), jnp.float32)
    sums = weigh([sim_ref[...]], per_sim, sums)
    sums = weigh([real_ref[...]], per_real, sums)

    def visit(distance, sums, keep_on):
        for kind, slots, scale in ((SIM, sims, per_sim), (REAL, reals, per_real)):
            for way in (RIGHTWARD, LEFTWARD):
                ring_copy(way, kind, distance).wait_recv()
                if keep_on or way == kind:
                    ring_copy(way, kind, distance + 1).start()
            if kind == SIM:
                sums = weigh([slots[distance - 1].reshape(2 * rows, width)], scale, sums)
            else:
                sums = weigh([slots[distance - 1, 0], slots[distance - 1, 1]], scale, sums)
        return sums

    if half <= 4:
        for distance in range(1, half - 1):
            sums = visit(distance, sums, True)
    else:
        sums = lax.fori_loop(1, half - 1, lambda d, s: visit(d, s, True), sums)
    sums = visit(half - 1, sums, False)

    ring_copy(RIGHTWARD, SIM, half).wait_recv()
    sums = weigh([sims[half - 1, RIGHTWARD]], per_sim, sums)
    ring_copy(LEFTWARD, REAL, half).wait_recv()
    sums = weigh([reals[half - 1, LEFTWARD]], per_real, sums)

    result = everyone.astype(jnp.float32) * sums + total[...]
    partial[...] = result[rows:]
    send_back = pltpu.make_async_remote_copy(
        src_ref=partial, dst_ref=arrived, send_sem=near_send.at[1], recv_sem=near_recv.at[1],
        device_id={"blk": sibling}, device_id_type=MESH,
    )
    send_back.start()
    send_back.wait_recv()
    out_ref[...] = result[:rows] + arrived[...]

    own_rows.wait_send()
    send_back.wait_send()
    for kind in (SIM, REAL):
        for way in (RIGHTWARD, LEFTWARD):
            last = half if way == kind else half - 1

            def sent(distance, unused):
                ring_copy(way, kind, distance).wait_send()
                return unused

            if half <= 4:
                for distance in range(1, last + 1):
                    sent(distance, 0)
            else:
                sent(1, 0)
                lax.fori_loop(2, last + 1, sent, 0)


def shards(sim_embed, real_embed):
    devices = lax.axis_size("blk")
    chips = devices // CORES
    half = chips // 2
    rows, width = sim_embed.shape
    rows_real = real_embed.shape[0]
    pairs = CORES * rows * (rows + rows_real) * chips
    return pl.pallas_call(
        functools.partial(kernel, chips, rows * devices, rows_real * devices),
        out_shape=jax.ShapeDtypeStruct((rows, width), jnp.float32),
        in_specs=[pl.BlockSpec(memory_space=pltpu.VMEM)] * 2,
        out_specs=pl.BlockSpec(memory_space=pltpu.VMEM),
        scratch_shapes=[
            pltpu.VMEM((half, 2, rows, width), jnp.bfloat16),
            pltpu.VMEM((half, 2, rows_real, width), jnp.bfloat16),
            pltpu.VMEM((CORES, rows, width), jnp.bfloat16),
            pltpu.VMEM((CORES * rows, width), jnp.float32),
            pltpu.VMEM((rows, width), jnp.float32),
            pltpu.VMEM((rows, width), jnp.float32),
            pltpu.SemaphoreType.DMA((2, 2, half)),
            pltpu.SemaphoreType.DMA((2, 2, half)),
            pltpu.SemaphoreType.DMA((2,)),
            pltpu.SemaphoreType.DMA((2,)),
        ],
        compiler_params=pltpu.CompilerParams(
            collective_id=0, has_side_effects=True, vmem_limit_bytes=48 * 1024 * 1024
        ),
        cost_estimate=pl.CostEstimate(
            flops=4 * pairs * width, bytes_accessed=6 * rows * width, transcendentals=pairs
        ),
    )(sim_embed, real_embed)


def solution(mesh):
    in_specs = (P(("grp", "blk"), None), P(("grp", "blk"), None))
    out_specs = P(("grp", "blk"), None)
    return jax.shard_map(shards, mesh=mesh, in_specs=in_specs, out_specs=out_specs, check_vma=False)
```

```python
import functools
import math

import jax
import jax.numpy as jnp
from jax import lax
from jax.experimental import pallas as pl
from jax.experimental.pallas import tpu as pltpu
from jax.sharding import PartitionSpec as P

MESH = pl.DeviceIdType.MESH
CORES = 2
RIGHTWARD, LEFTWARD = 0, 1
ORDER = ((0, 2, 1, 3), (1, 3, 0, 2))
PIECES = 4
AHEAD = 2


def grid_sides(chips):
    inner = max(k for k in range(2, chips + 1, 2) if k * k <= chips and chips % k == 0)
    return chips // inner, inner


def place_on_cycle(chip, outer, inner):
    z, y = chip // inner, chip % inner
    run = outer - 1
    down = (z - 1) + (y % 2) * (outer - 2 * z)
    back = 1 + inner * run + (inner - 1 - y)
    return jnp.where(z > 0, 1 + y * run + down, jnp.where(y == 0, 0, back))


def chip_on_cycle(place, outer, inner):
    run = outer - 1
    q = jnp.maximum(place - 1, 0)
    y, r = q // run, q % run
    z = 1 + r + (y % 2) * (outer - 2 - 2 * r)
    back = inner - 1 - (q - inner * run)
    inside = z * inner + y
    return jnp.where(place == 0, 0, jnp.where(q < inner * run, inside, back))


def kernel(
    chips, count_sim, count_real,
    sim_ref, real_ref, out_ref,
    sims, reals, query, own_real, total, partial, arrived,
    send_sem, recv_sem, near_send, near_recv, fetch_sem,
):
    half = chips // 2
    outer, inner = grid_sides(chips)
    rows, width = sim_ref.shape
    me = lax.axis_index("blk")
    core = me % CORES
    place = place_on_cycle(me // CORES, outer, inner)
    right = chip_on_cycle((place + 1) % chips, outer, inner) * CORES + core
    left = chip_on_cycle((place + chips - 1) % chips, outer, inner) * CORES + core
    sibling = me + 1 - 2 * core

    barrier = pltpu.get_barrier_semaphore()
    for other in (left, right, sibling):
        pl.semaphore_signal(barrier, inc=1, device_id={"blk": other}, device_id_type=MESH)
    pl.semaphore_wait(barrier, 3)

    def part(ref, piece):
        if piece < 2:
            return ref.at[pl.ds(piece * (rows // 2), rows // 2), :]
        return ref.at[:, pl.ds((piece - 2) * (width // 2), width // 2)]

    def ring_copy(way, turn, distance, leaving=True):
        piece = ORDER[way][turn]
        own, slots = (sim_ref, sims) if piece < 2 else (real_ref, reals)
        first = isinstance(distance, int) and distance == 1
        last = isinstance(distance, int) and distance == half
        if not leaving:
            source = slots.at[distance - 1, way]
        else:
            source = own if first else slots.at[distance - 2, way]
        return pltpu.make_async_remote_copy(
            src_ref=part(source, piece),
            dst_ref=part(slots.at[distance - 1, 0 if last else way], piece),
            send_sem=send_sem.at[way, piece, distance - 1],
            recv_sem=recv_sem.at[way, piece, distance - 1],
            device_id={"blk": right if way == RIGHTWARD else left},
            device_id_type=MESH,
        )

    own_rows = pltpu.make_async_remote_copy(
        src_ref=sim_ref, dst_ref=query.at[1], send_sem=near_send.at[0], recv_sem=near_recv.at[0],
        device_id={"blk": sibling}, device_id_type=MESH,
    )
    def was_sent(way, turn, distance):
        ring_copy(way, turn, distance, leaving=False).wait_send()

    def send(turn, distance, ways=(RIGHTWARD, LEFTWARD)):
        for way in ways:
            if turn >= AHEAD:
                was_sent(way, turn - AHEAD, distance)
            elif not (isinstance(distance, int) and distance == 1):
                was_sent(way, turn + PIECES - AHEAD, distance - 1)
            ring_copy(way, turn, distance).start()

    for turn in range(AHEAD):
        send(turn, 1)
    own_rows.start()
    fetch_sim = pltpu.make_async_copy(sim_ref, query.at[0], fetch_sem.at[0])
    fetch_real = pltpu.make_async_copy(real_ref, own_real, fetch_sem.at[1])
    fetch_sim.start()
    fetch_real.start()
    for turn in range(AHEAD, PIECES):
        send(turn, 1)

    rate = 0.125 / width * math.log2(math.e)

    def row_norms(block):
        values = block.astype(jnp.float32)
        return jnp.sum(values * values, axis=1, keepdims=True) * rate

    def across(column):
        return jnp.transpose(jnp.broadcast_to(column, (column.shape[0], 128)))[0:1]

    def pull(rows_b, rows_norm, keys, scale):
        gram = lax.dot_general(
            rows_b, keys, (((1,), (1,)), ((), ())), preferred_element_type=jnp.float32
        )
        e1 = jnp.exp2((2.0 * rate) * gram - (rows_norm + across(row_norms(keys))))
        e2 = e1 * e1
        e4 = e2 * e2
        e8 = e4 * e4
        weight = 0.125 * e1 + 0.25 * e2 + 0.5 * e4 + e8 + 2.0 * (e8 * e8)
        pulled = jnp.dot(weight.astype(jnp.bfloat16), keys, preferred_element_type=jnp.float32)
        return jnp.sum(weight, axis=1, keepdims=True) * scale, pulled * scale

    fetch_sim.wait()
    fetch_real.wait()
    own_rows.wait_recv()
    everyone = query[...].reshape(CORES * rows, width)
    every_norm = row_norms(everyone)

    def weigh(blocks, scale, sums):
        for keys in blocks:
            summed, pulled = pull(everyone, every_norm, keys, scale)
            total[...] -= pulled
            sums = sums + summed
        return sums

    per_sim, per_real = -1.0 / count_sim, 1.0 / count_real
    total[...] = jnp.zeros_like(total)
    sums = jnp.zeros((CORES * rows, 1), jnp.float32)
    sums = weigh([query[0]], per_sim, sums)
    sums = weigh([own_real[...]], per_real, sums)

    def visit(distance, sums, keep_on):
        for turn in range(PIECES):
            for way in (RIGHTWARD, LEFTWARD):
                ring_copy(way, turn, distance, leaving=False).wait_recv()
                if keep_on or turn < PIECES // 2:
                    send(turn, distance + 1, (way,))
            if turn == 2:
                sums = weigh([sims[distance - 1].reshape(2 * rows, width)], per_sim, sums)
        return weigh([reals[distance - 1, 0], reals[distance - 1, 1]], per_real, sums)

    if half <= 4:
        for distance in range(1, half - 1):
            sums = visit(distance, sums, True)
    else:
        sums = lax.fori_loop(1, half - 1, lambda d, s: visit(d, s, True), sums)
    sums = visit(half - 1, sums, False)

    for way in (RIGHTWARD, LEFTWARD):
        ring_copy(way, 0, half).wait_recv()
    sums = weigh([sims[half - 1, 0]], per_sim, sums)
    for way in (RIGHTWARD, LEFTWARD):
        ring_copy(way, 1, half).wait_recv()

    def finish(begin):
        span = slice(begin, begin + rows)
        summed, pulled = pull(everyone[span], every_norm[span], reals[half - 1, 0], per_real)
        values = everyone[span].astype(jnp.float32)
        return values * (sums[span] + summed) + (total[span] - pulled)

    partial[...] = finish(rows)
    send_back = pltpu.make_async_remote_copy(
        src_ref=partial, dst_ref=arrived, send_sem=near_send.at[1], recv_sem=near_recv.at[1],
        device_id={"blk": sibling}, device_id_type=MESH,
    )
    send_back.start()
    out_ref[...] = finish(0)

    own_rows.wait_send()
    for way in (RIGHTWARD, LEFTWARD):
        for turn in range(PIECES // 2 - AHEAD, PIECES // 2):
            was_sent(way, turn, half)
    send_back.wait_recv()
    out_ref[...] += arrived[...]
    send_back.wait_send()


def shards(sim_embed, real_embed):
    devices = lax.axis_size("blk")
    chips = devices // CORES
    half = chips // 2
    rows, width = sim_embed.shape
    rows_real = real_embed.shape[0]
    pairs = CORES * rows * (rows + rows_real) * chips
    return pl.pallas_call(
        functools.partial(kernel, chips, rows * devices, rows_real * devices),
        out_shape=jax.ShapeDtypeStruct((rows, width), jnp.float32),
        in_specs=[pl.BlockSpec(memory_space=pltpu.HBM)] * 2,
        out_specs=pl.BlockSpec(memory_space=pltpu.VMEM),
        scratch_shapes=[
            pltpu.VMEM((half, 2, rows, width), jnp.bfloat16),
            pltpu.VMEM((half, 2, rows_real, width), jnp.bfloat16),
            pltpu.VMEM((CORES, rows, width), jnp.bfloat16),
            pltpu.VMEM((rows_real, width), jnp.bfloat16),
            pltpu.VMEM((CORES * rows, width), jnp.float32),
            pltpu.VMEM((rows, width), jnp.float32),
            pltpu.VMEM((rows, width), jnp.float32),
            pltpu.SemaphoreType.DMA((2, PIECES, half)),
            pltpu.SemaphoreType.DMA((2, PIECES, half)),
            pltpu.SemaphoreType.DMA((2,)),
            pltpu.SemaphoreType.DMA((2,)),
            pltpu.SemaphoreType.DMA((2,)),
        ],
        compiler_params=pltpu.CompilerParams(
            collective_id=0, has_side_effects=True, vmem_limit_bytes=48 * 1024 * 1024
        ),
        cost_estimate=pl.CostEstimate(
            flops=4 * pairs * width, bytes_accessed=6 * rows * width, transcendentals=pairs
        ),
    )(*(pltpu.with_memory_space_constraint(x, pltpu.HBM) for x in (sim_embed, real_embed)))


def solution(mesh):
    in_specs = (P(("grp", "blk"), None), P(("grp", "blk"), None))
    out_specs = P(("grp", "blk"), None)
    return jax.shard_map(shards, mesh=mesh, in_specs=in_specs, out_specs=out_specs, check_vma=False)
```

```python
import functools
import math

import jax
import jax.numpy as jnp
from jax import lax
from jax.experimental import pallas as pl
from jax.experimental.pallas import tpu as pltpu
from jax.sharding import PartitionSpec as P

MESH = pl.DeviceIdType.MESH
CORES = 2
RIGHTWARD, LEFTWARD = 0, 1
ORDER = ((0, 2, 1, 3), (1, 3, 0, 2))
PIECES = 4
AHEAD = 3


def grid_sides(chips):
    inner = max(k for k in range(2, chips + 1, 2) if k * k <= chips and chips % k == 0)
    return chips // inner, inner


def place_on_cycle(chip, outer, inner):
    z, y = chip // inner, chip % inner
    run = outer - 1
    down = (z - 1) + (y % 2) * (outer - 2 * z)
    back = 1 + inner * run + (inner - 1 - y)
    return jnp.where(z > 0, 1 + y * run + down, jnp.where(y == 0, 0, back))


def chip_on_cycle(place, outer, inner):
    run = outer - 1
    q = jnp.maximum(place - 1, 0)
    y, r = q // run, q % run
    z = 1 + r + (y % 2) * (outer - 2 - 2 * r)
    back = inner - 1 - (q - inner * run)
    inside = z * inner + y
    return jnp.where(place == 0, 0, jnp.where(q < inner * run, inside, back))


def kernel(
    chips, count_sim, count_real,
    sim_ref, real_ref, out_ref,
    sims, reals, query, own_real, total, partial, arrived,
    send_sem, recv_sem, near_send, near_recv, fetch_sem,
):
    half = chips // 2
    outer, inner = grid_sides(chips)
    rows, width = sim_ref.shape
    me = lax.axis_index("blk")
    core = me % CORES
    place = place_on_cycle(me // CORES, outer, inner)
    right = chip_on_cycle((place + 1) % chips, outer, inner) * CORES + core
    left = chip_on_cycle((place + chips - 1) % chips, outer, inner) * CORES + core
    sibling = me + 1 - 2 * core

    barrier = pltpu.get_barrier_semaphore()
    for other in (left, right, sibling):
        pl.semaphore_signal(barrier, inc=1, device_id={"blk": other}, device_id_type=MESH)
    fetch_sim = pltpu.make_async_copy(sim_ref, query.at[0], fetch_sem.at[0])
    fetch_real = pltpu.make_async_copy(real_ref, own_real, fetch_sem.at[1])
    fetch_sim.start()
    fetch_real.start()
    fetch_sim.wait()
    fetch_real.wait()
    pl.semaphore_wait(barrier, 3)

    def part(ref, piece):
        if piece < 2:
            return ref.at[pl.ds(piece * (rows // 2), rows // 2), :]
        return ref.at[:, pl.ds((piece - 2) * (width // 2), width // 2)]

    def ring_copy(way, turn, distance, leaving=True):
        piece = ORDER[way][turn]
        own, slots = (query.at[0], sims) if piece < 2 else (own_real, reals)
        first = isinstance(distance, int) and distance == 1
        last = isinstance(distance, int) and distance == half
        if not leaving:
            source = slots.at[distance - 1, way]
        else:
            source = own if first else slots.at[distance - 2, way]
        return pltpu.make_async_remote_copy(
            src_ref=part(source, piece),
            dst_ref=part(slots.at[distance - 1, 0 if last else way], piece),
            send_sem=send_sem.at[way, piece, distance - 1],
            recv_sem=recv_sem.at[way, piece, distance - 1],
            device_id={"blk": right if way == RIGHTWARD else left},
            device_id_type=MESH,
        )

    own_rows = pltpu.make_async_remote_copy(
        src_ref=query.at[0], dst_ref=query.at[1], send_sem=near_send.at[0], recv_sem=near_recv.at[0],
        device_id={"blk": sibling}, device_id_type=MESH,
    )
    def was_sent(way, turn, distance):
        ring_copy(way, turn, distance, leaving=False).wait_send()

    def send(turn, distance, ways=(RIGHTWARD, LEFTWARD)):
        for way in ways:
            if turn >= AHEAD:
                was_sent(way, turn - AHEAD, distance)
            elif not (isinstance(distance, int) and distance == 1):
                was_sent(way, turn + PIECES - AHEAD, distance - 1)
            ring_copy(way, turn, distance).start()

    for turn in range(AHEAD):
        send(turn, 1)
    own_rows.start()
    for turn in range(AHEAD, PIECES):
        send(turn, 1)

    rate = 0.125 / width * math.log2(math.e)

    def row_norms(block):
        values = block.astype(jnp.float32)
        return jnp.sum(values * values, axis=1, keepdims=True) * rate

    def across(column):
        return jnp.transpose(jnp.broadcast_to(column, (column.shape[0], 128)))[0:1]

    def pull(rows_b, rows_norm, keys, scale):
        gram = lax.dot_general(
            rows_b, keys, (((1,), (1,)), ((), ())), preferred_element_type=jnp.float32
        )
        e1 = jnp.exp2((2.0 * rate) * gram - (rows_norm + across(row_norms(keys))))
        e2 = e1 * e1
        e4 = e2 * e2
        e8 = e4 * e4
        weight = 0.125 * e1 + 0.25 * e2 + 0.5 * e4 + e8 + 2.0 * (e8 * e8)
        pulled = jnp.dot(weight.astype(jnp.bfloat16), keys, preferred_element_type=jnp.float32)
        return jnp.sum(weight, axis=1, keepdims=True) * scale, pulled * scale

    own_rows.wait_recv()
    everyone = query[...].reshape(CORES * rows, width)
    every_norm = row_norms(everyone)

    def weigh(blocks, scale, sums):
        for keys in blocks:
            summed, pulled = pull(everyone, every_norm, keys, scale)
            total[...] -= pulled
            sums = sums + summed
        return sums

    per_sim, per_real = -1.0 / count_sim, 1.0 / count_real
    total[...] = jnp.zeros_like(total)
    sums = jnp.zeros((CORES * rows, 1), jnp.float32)
    sums = weigh([query[0]], per_sim, sums)
    sums = weigh([own_real[...]], per_real, sums)

    def visit(distance, sums, keep_on):
        for turn in range(PIECES):
            for way in (RIGHTWARD, LEFTWARD):
                ring_copy(way, turn, distance, leaving=False).wait_recv()
                if keep_on or turn < PIECES // 2:
                    send(turn, distance + 1, (way,))
            if turn == 2:
                sums = weigh([sims[distance - 1].reshape(2 * rows, width)], per_sim, sums)
        return weigh([reals[distance - 1, 0], reals[distance - 1, 1]], per_real, sums)

    if half <= 4:
        for distance in range(1, half - 1):
            sums = visit(distance, sums, True)
    else:
        sums = lax.fori_loop(1, half - 1, lambda d, s: visit(d, s, True), sums)
    sums = visit(half - 1, sums, False)

    for way in (RIGHTWARD, LEFTWARD):
        ring_copy(way, 0, half).wait_recv()
    sums = weigh([sims[half - 1, 0]], per_sim, sums)
    for way in (RIGHTWARD, LEFTWARD):
        ring_copy(way, 1, half).wait_recv()

    def finish(begin):
        span = slice(begin, begin + rows)
        summed, pulled = pull(everyone[span], every_norm[span], reals[half - 1, 0], per_real)
        values = everyone[span].astype(jnp.float32)
        return values * (sums[span] + summed) + (total[span] - pulled)

    partial[...] = finish(rows)
    send_back = pltpu.make_async_remote_copy(
        src_ref=partial, dst_ref=arrived, send_sem=near_send.at[1], recv_sem=near_recv.at[1],
        device_id={"blk": sibling}, device_id_type=MESH,
    )
    send_back.start()
    out_ref[...] = finish(0)

    own_rows.wait_send()
    for way in (RIGHTWARD, LEFTWARD):
        for behind in range(AHEAD):
            turn = PIECES // 2 - 1 - behind
            was_sent(way, turn % PIECES, half if turn >= 0 else half - 1)
    send_back.wait_recv()
    out_ref[...] += arrived[...]
    send_back.wait_send()


def shards(sim_embed, real_embed):
    devices = lax.axis_size("blk")
    chips = devices // CORES
    half = chips // 2
    rows, width = sim_embed.shape
    rows_real = real_embed.shape[0]
    pairs = CORES * rows * (rows + rows_real) * chips
    return pl.pallas_call(
        functools.partial(kernel, chips, rows * devices, rows_real * devices),
        out_shape=jax.ShapeDtypeStruct((rows, width), jnp.float32),
        in_specs=[pl.BlockSpec(memory_space=pltpu.HBM)] * 2,
        out_specs=pl.BlockSpec(memory_space=pltpu.VMEM),
        scratch_shapes=[
            pltpu.VMEM((half, 2, rows, width), jnp.bfloat16),
            pltpu.VMEM((half, 2, rows_real, width), jnp.bfloat16),
            pltpu.VMEM((CORES, rows, width), jnp.bfloat16),
            pltpu.VMEM((rows_real, width), jnp.bfloat16),
            pltpu.VMEM((CORES * rows, width), jnp.float32),
            pltpu.VMEM((rows, width), jnp.float32),
            pltpu.VMEM((rows, width), jnp.float32),
            pltpu.SemaphoreType.DMA((2, PIECES, half)),
            pltpu.SemaphoreType.DMA((2, PIECES, half)),
            pltpu.SemaphoreType.DMA((2,)),
            pltpu.SemaphoreType.DMA((2,)),
            pltpu.SemaphoreType.DMA((2,)),
        ],
        compiler_params=pltpu.CompilerParams(
            collective_id=0, has_side_effects=True, vmem_limit_bytes=48 * 1024 * 1024
        ),
        cost_estimate=pl.CostEstimate(
            flops=4 * pairs * width, bytes_accessed=6 * rows * width, transcendentals=pairs
        ),
    )(*(pltpu.with_memory_space_constraint(x, pltpu.HBM) for x in (sim_embed, real_embed)))


def solution(mesh):
    in_specs = (P(("grp", "blk"), None), P(("grp", "blk"), None))
    out_specs = P(("grp", "blk"), None)
    return jax.shard_map(shards, mesh=mesh, in_specs=in_specs, out_specs=out_specs, check_vma=False)
```

```python
import functools
import math

import jax
import jax.numpy as jnp
from jax import lax
from jax.experimental import pallas as pl
from jax.experimental.pallas import tpu as pltpu
from jax.sharding import PartitionSpec as P

MESH = pl.DeviceIdType.MESH
CORES = 2
RIGHTWARD, LEFTWARD = 0, 1
ORDER = ((0, 2, 1, 3), (1, 3, 0, 2))
PIECES = 4
AHEAD = 3


def grid_sides(chips):
    inner = max(k for k in range(2, chips + 1, 2) if k * k <= chips and chips % k == 0)
    return chips // inner, inner


def place_on_cycle(chip, outer, inner):
    z, y = chip // inner, chip % inner
    run = outer - 1
    down = (z - 1) + (y % 2) * (outer - 2 * z)
    back = 1 + inner * run + (inner - 1 - y)
    return jnp.where(z > 0, 1 + y * run + down, jnp.where(y == 0, 0, back))


def chip_on_cycle(place, outer, inner):
    run = outer - 1
    q = jnp.maximum(place - 1, 0)
    y, r = q // run, q % run
    z = 1 + r + (y % 2) * (outer - 2 - 2 * r)
    back = inner - 1 - (q - inner * run)
    inside = z * inner + y
    return jnp.where(place == 0, 0, jnp.where(q < inner * run, inside, back))


def kernel(
    chips, count_sim, count_real,
    sim_ref, real_ref, out_ref,
    sims, reals, query, own_real, total, partial, arrived,
    send_sem, recv_sem, near_send, near_recv, fetch_sem, pass_send, pass_recv, other_keys,
):
    half = chips // 2
    outer, inner = grid_sides(chips)
    rows, width = sim_ref.shape
    me = lax.axis_index("blk")
    core = me % CORES
    place = place_on_cycle(me // CORES, outer, inner)
    right = chip_on_cycle((place + 1) % chips, outer, inner) * CORES + core
    left = chip_on_cycle((place + chips - 1) % chips, outer, inner) * CORES + core
    sibling = me + 1 - 2 * core

    barrier = pltpu.get_barrier_semaphore()
    for other in (left, right, sibling):
        pl.semaphore_signal(barrier, inc=1, device_id={"blk": other}, device_id_type=MESH)
    fetch_sim = pltpu.make_async_copy(sim_ref, query.at[0], fetch_sem.at[0])
    fetch_real = pltpu.make_async_copy(real_ref, own_real, fetch_sem.at[1])
    fetch_sim.start()
    fetch_real.start()
    fetch_sim.wait()
    fetch_real.wait()
    pl.semaphore_wait(barrier, 3)

    def part(ref, piece):
        if piece < 2:
            return ref.at[pl.ds(piece * (rows // 2), rows // 2), :]
        return ref.at[:, pl.ds((piece - 2) * (width // 2), width // 2)]

    def ring_copy(way, turn, distance, leaving=True):
        piece = ORDER[way][turn]
        own, slots = (query.at[0], sims) if piece < 2 else (own_real, reals)
        first = isinstance(distance, int) and distance == 1
        last = isinstance(distance, int) and distance == half
        if not leaving:
            source = slots.at[distance - 1, way]
        else:
            source = own if first else slots.at[distance - 2, way]
        return pltpu.make_async_remote_copy(
            src_ref=part(source, piece),
            dst_ref=part(slots.at[distance - 1, 0 if last else way], piece),
            send_sem=send_sem.at[way, piece, distance - 1],
            recv_sem=recv_sem.at[way, piece, distance - 1],
            device_id={"blk": right if way == RIGHTWARD else left},
            device_id_type=MESH,
        )

    own_rows = pltpu.make_async_remote_copy(
        src_ref=query.at[0], dst_ref=query.at[1], send_sem=near_send.at[0], recv_sem=near_recv.at[0],
        device_id={"blk": sibling}, device_id_type=MESH,
    )
    def was_sent(way, turn, distance):
        ring_copy(way, turn, distance, leaving=False).wait_send()

    def send(turn, distance, ways=(RIGHTWARD, LEFTWARD)):
        for way in ways:
            if turn >= AHEAD:
                was_sent(way, turn - AHEAD, distance)
            elif not (isinstance(distance, int) and distance == 1):
                was_sent(way, turn + PIECES - AHEAD, distance - 1)
            ring_copy(way, turn, distance).start()

    for turn in range(AHEAD):
        send(turn, 1)
    own_rows.start()
    for turn in range(AHEAD, PIECES):
        send(turn, 1)

    rate = 0.125 / width * math.log2(math.e)

    def row_norms(block):
        values = block.astype(jnp.float32)
        return jnp.sum(values * values, axis=1, keepdims=True) * rate

    def across(column):
        return jnp.transpose(jnp.broadcast_to(column, (column.shape[0], 128)))[0:1]

    def pull(rows_b, rows_norm, keys, scale):
        gram = lax.dot_general(
            rows_b, keys, (((1,), (1,)), ((), ())), preferred_element_type=jnp.float32
        )
        e1 = jnp.exp2((2.0 * rate) * gram - (rows_norm + across(row_norms(keys))))
        e2 = e1 * e1
        e4 = e2 * e2
        e8 = e4 * e4
        weight = 0.125 * e1 + 0.25 * e2 + 0.5 * e4 + e8 + 2.0 * (e8 * e8)
        pulled = jnp.dot(weight.astype(jnp.bfloat16), keys, preferred_element_type=jnp.float32)
        return jnp.sum(weight, axis=1, keepdims=True) * scale, pulled * scale

    own_rows.wait_recv()
    everyone = query[...].reshape(CORES * rows, width)
    every_norm = row_norms(everyone)

    def weigh(blocks, scale, sums):
        for keys in blocks:
            summed, pulled = pull(everyone, every_norm, keys, scale)
            total[...] -= pulled
            sums = sums + summed
        return sums

    per_sim, per_real = -1.0 / count_sim, 1.0 / count_real
    total[...] = jnp.zeros_like(total)
    sums = jnp.zeros((CORES * rows, 1), jnp.float32)
    sums = weigh([query[0]], per_sim, sums)
    sums = weigh([own_real[...]], per_real, sums)

    def visit(distance, sums, keep_on):
        for turn in range(PIECES):
            for way in (RIGHTWARD, LEFTWARD):
                ring_copy(way, turn, distance, leaving=False).wait_recv()
                if keep_on or turn < PIECES // 2:
                    send(turn, distance + 1, (way,))
            if turn == 2:
                sums = weigh([sims[distance - 1].reshape(2 * rows, width)], per_sim, sums)
        return weigh([reals[distance - 1, 0], reals[distance - 1, 1]], per_real, sums)

    if half <= 4:
        for distance in range(1, half - 1):
            sums = visit(distance, sums, True)
    else:
        sums = lax.fori_loop(1, half - 1, lambda d, s: visit(d, s, True), sums)
    sums = visit(half - 1, sums, False)

    for way in (RIGHTWARD, LEFTWARD):
        ring_copy(way, 0, half).wait_recv()
    sums = weigh([sims[half - 1, 0]], per_sim, sums)
    result = everyone.astype(jnp.float32) * sums + total[...]
    partial[...] = result[rows:]
    send_back = pltpu.make_async_remote_copy(
        src_ref=partial, dst_ref=arrived, send_sem=near_send.at[1], recv_sem=near_recv.at[1],
        device_id={"blk": sibling}, device_id_type=MESH,
    )
    send_back.start()

    def pass_on(way):
        lanes = pl.ds(way * (width // 2), width // 2)
        return pltpu.make_async_remote_copy(
            src_ref=reals.at[half - 1, 0, :, lanes], dst_ref=other_keys.at[:, lanes],
            send_sem=pass_send.at[way], recv_sem=pass_recv.at[way],
            device_id={"blk": sibling}, device_id_type=MESH,
        )

    for way in (RIGHTWARD, LEFTWARD):
        ring_copy(way, 1, half).wait_recv()
        pass_on(way).start()

    mine = everyone[:rows]
    mine_f = mine.astype(jnp.float32)

    def last_term(keys):
        summed, pulled = pull(mine, every_norm[:rows], keys, per_real)
        return mine_f * summed - pulled

    out_ref[...] = result[:rows] + last_term(reals[half - 1, 0])
    send_back.wait_recv()
    out_ref[...] += arrived[...]

    own_rows.wait_send()
    for way in (RIGHTWARD, LEFTWARD):
        for behind in range(AHEAD):
            turn = PIECES // 2 - 1 - behind
            was_sent(way, turn % PIECES, half if turn >= 0 else half - 1)
    send_back.wait_send()
    for way in (RIGHTWARD, LEFTWARD):
        pass_on(way).wait_recv()
    out_ref[...] += last_term(other_keys[...])
    for way in (RIGHTWARD, LEFTWARD):
        pass_on(way).wait_send()


def shards(sim_embed, real_embed):
    devices = lax.axis_size("blk")
    chips = devices // CORES
    half = chips // 2
    rows, width = sim_embed.shape
    rows_real = real_embed.shape[0]
    pairs = CORES * rows * (rows + rows_real) * chips
    return pl.pallas_call(
        functools.partial(kernel, chips, rows * devices, rows_real * devices),
        out_shape=jax.ShapeDtypeStruct((rows, width), jnp.float32),
        in_specs=[pl.BlockSpec(memory_space=pltpu.HBM)] * 2,
        out_specs=pl.BlockSpec(memory_space=pltpu.VMEM),
        scratch_shapes=[
            pltpu.VMEM((half, 2, rows, width), jnp.bfloat16),
            pltpu.VMEM((half, 2, rows_real, width), jnp.bfloat16),
            pltpu.VMEM((CORES, rows, width), jnp.bfloat16),
            pltpu.VMEM((rows_real, width), jnp.bfloat16),
            pltpu.VMEM((CORES * rows, width), jnp.float32),
            pltpu.VMEM((rows, width), jnp.float32),
            pltpu.VMEM((rows, width), jnp.float32),
            pltpu.SemaphoreType.DMA((2, PIECES, half)),
            pltpu.SemaphoreType.DMA((2, PIECES, half)),
            pltpu.SemaphoreType.DMA((2,)),
            pltpu.SemaphoreType.DMA((2,)),
            pltpu.SemaphoreType.DMA((2,)),
            pltpu.SemaphoreType.DMA((2,)),
            pltpu.SemaphoreType.DMA((2,)),
            pltpu.VMEM((rows_real, width), jnp.bfloat16),
        ],
        compiler_params=pltpu.CompilerParams(
            collective_id=0, has_side_effects=True, vmem_limit_bytes=48 * 1024 * 1024
        ),
        cost_estimate=pl.CostEstimate(
            flops=4 * pairs * width, bytes_accessed=6 * rows * width, transcendentals=pairs
        ),
    )(*(pltpu.with_memory_space_constraint(x, pltpu.HBM) for x in (sim_embed, real_embed)))


def solution(mesh):
    in_specs = (P(("grp", "blk"), None), P(("grp", "blk"), None))
    out_specs = P(("grp", "blk"), None)
    return jax.shard_map(shards, mesh=mesh, in_specs=in_specs, out_specs=out_specs, check_vma=False)
```

```python
import functools
import math

import jax
import jax.numpy as jnp
from jax import lax
from jax.experimental import pallas as pl
from jax.experimental.pallas import tpu as pltpu
from jax.sharding import PartitionSpec as P

MESH = pl.DeviceIdType.MESH
CORES = 2
RIGHTWARD, LEFTWARD = 0, 1
ORDER = ((0, 2, 1, 3), (1, 3, 0, 2))
PIECES = 4
AHEAD = 3


def grid_sides(chips):
    inner = max(k for k in range(2, chips + 1, 2) if k * k <= chips and chips % k == 0)
    return chips // inner, inner


def place_on_cycle(chip, outer, inner):
    z, y = chip // inner, chip % inner
    run = outer - 1
    down = (z - 1) + (y % 2) * (outer - 2 * z)
    back = 1 + inner * run + (inner - 1 - y)
    return jnp.where(z > 0, 1 + y * run + down, jnp.where(y == 0, 0, back))


def chip_on_cycle(place, outer, inner):
    run = outer - 1
    q = jnp.maximum(place - 1, 0)
    y, r = q // run, q % run
    z = 1 + r + (y % 2) * (outer - 2 - 2 * r)
    back = inner - 1 - (q - inner * run)
    inside = z * inner + y
    return jnp.where(place == 0, 0, jnp.where(q < inner * run, inside, back))


def kernel(
    chips, count_sim, count_real,
    sim_ref, real_ref, out_ref,
    sims, reals, query, own_real, total, partial, arrived,
    send_sem, recv_sem, near_send, near_recv, fetch_sem,
):
    half = chips // 2
    outer, inner = grid_sides(chips)
    rows, width = sim_ref.shape
    me = lax.axis_index("blk")
    core = me % CORES
    place = place_on_cycle(me // CORES, outer, inner)
    right = chip_on_cycle((place + 1) % chips, outer, inner) * CORES + core
    left = chip_on_cycle((place + chips - 1) % chips, outer, inner) * CORES + core
    sibling = me + 1 - 2 * core

    barrier = pltpu.get_barrier_semaphore()
    for other in (left, right, sibling):
        pl.semaphore_signal(barrier, inc=1, device_id={"blk": other}, device_id_type=MESH)
    fetch_sim = pltpu.make_async_copy(sim_ref, query.at[0], fetch_sem.at[0])
    fetch_real = pltpu.make_async_copy(real_ref, own_real, fetch_sem.at[1])
    fetch_sim.start()
    fetch_real.start()
    pl.semaphore_wait(barrier, 3)
    fetch_sim.wait()

    def part(ref, piece):
        if piece < 2:
            return ref.at[pl.ds(piece * (rows // 2), rows // 2), :]
        return ref.at[:, pl.ds((piece - 2) * (width // 2), width // 2)]

    def ring_copy(way, turn, distance, leaving=True):
        piece = ORDER[way][turn]
        own, slots = (query.at[0], sims) if piece < 2 else (own_real, reals)
        first = isinstance(distance, int) and distance == 1
        last = isinstance(distance, int) and distance == half
        if not leaving:
            source = slots.at[distance - 1, way]
        else:
            source = own if first else slots.at[distance - 2, way]
        return pltpu.make_async_remote_copy(
            src_ref=part(source, piece),
            dst_ref=part(slots.at[distance - 1, 0 if last else way], piece),
            send_sem=send_sem.at[way, piece, distance - 1],
            recv_sem=recv_sem.at[way, piece, distance - 1],
            device_id={"blk": right if way == RIGHTWARD else left},
            device_id_type=MESH,
        )

    own_rows = pltpu.make_async_remote_copy(
        src_ref=query.at[0], dst_ref=query.at[1], send_sem=near_send.at[0], recv_sem=near_recv.at[0],
        device_id={"blk": sibling}, device_id_type=MESH,
    )
    def was_sent(way, turn, distance):
        ring_copy(way, turn, distance, leaving=False).wait_send()

    def send(turn, distance, ways=(RIGHTWARD, LEFTWARD)):
        for way in ways:
            if turn >= AHEAD:
                was_sent(way, turn - AHEAD, distance)
            elif not (isinstance(distance, int) and distance == 1):
                was_sent(way, turn + PIECES - AHEAD, distance - 1)
            ring_copy(way, turn, distance).start()

    send(0, 1)
    fetch_real.wait()
    for turn in range(1, AHEAD):
        send(turn, 1)
    own_rows.start()
    for turn in range(AHEAD, PIECES):
        send(turn, 1)

    rate = 0.125 / width * math.log2(math.e)

    def row_norms(block):
        values = block.astype(jnp.float32)
        return jnp.sum(values * values, axis=1, keepdims=True) * rate

    def across(column):
        return jnp.transpose(jnp.broadcast_to(column, (column.shape[0], 128)))[0:1]

    def pull(rows_b, rows_norm, keys, scale):
        gram = lax.dot_general(
            rows_b, keys, (((1,), (1,)), ((), ())), preferred_element_type=jnp.float32
        )
        e1 = jnp.exp2((2.0 * rate) * gram - (rows_norm + across(row_norms(keys))))
        e2 = e1 * e1
        e4 = e2 * e2
        e8 = e4 * e4
        weight = 0.125 * e1 + 0.25 * e2 + 0.5 * e4 + e8 + 2.0 * (e8 * e8)
        pulled = jnp.dot(weight.astype(jnp.bfloat16), keys, preferred_element_type=jnp.float32)
        return jnp.sum(weight, axis=1, keepdims=True) * scale, pulled * scale

    own_rows.wait_recv()
    everyone = query[...].reshape(CORES * rows, width)
    every_norm = row_norms(everyone)

    def weigh(blocks, scale, sums):
        for keys in blocks:
            summed, pulled = pull(everyone, every_norm, keys, scale)
            total[...] -= pulled
            sums = sums + summed
        return sums

    per_sim, per_real = -1.0 / count_sim, 1.0 / count_real
    total[...] = jnp.zeros_like(total)
    sums = jnp.zeros((CORES * rows, 1), jnp.float32)
    sums = weigh([query[0]], per_sim, sums)
    sums = weigh([own_real[...]], per_real, sums)

    def visit(distance, sums, keep_on):
        for turn in range(PIECES):
            for way in (RIGHTWARD, LEFTWARD):
                ring_copy(way, turn, distance, leaving=False).wait_recv()
                if keep_on or turn < PIECES // 2:
                    send(turn, distance + 1, (way,))
            if turn == 2:
                sums = weigh([sims[distance - 1].reshape(2 * rows, width)], per_sim, sums)
        return weigh([reals[distance - 1, 0], reals[distance - 1, 1]], per_real, sums)

    if half <= 4:
        for distance in range(1, half - 1):
            sums = visit(distance, sums, True)
    else:
        sums = lax.fori_loop(1, half - 1, lambda d, s: visit(d, s, True), sums)
    sums = visit(half - 1, sums, False)

    for way in (RIGHTWARD, LEFTWARD):
        ring_copy(way, 0, half).wait_recv()
    sums = weigh([sims[half - 1, 0]], per_sim, sums)
    for way in (RIGHTWARD, LEFTWARD):
        ring_copy(way, 1, half).wait_recv()

    def finish(begin):
        span = slice(begin, begin + rows)
        summed, pulled = pull(everyone[span], every_norm[span], reals[half - 1, 0], per_real)
        values = everyone[span].astype(jnp.float32)
        return values * (sums[span] + summed) + (total[span] - pulled)

    partial[...] = finish(rows)
    send_back = pltpu.make_async_remote_copy(
        src_ref=partial, dst_ref=arrived, send_sem=near_send.at[1], recv_sem=near_recv.at[1],
        device_id={"blk": sibling}, device_id_type=MESH,
    )
    send_back.start()
    out_ref[...] = finish(0)

    own_rows.wait_send()
    for way in (RIGHTWARD, LEFTWARD):
        for behind in range(AHEAD):
            turn = PIECES // 2 - 1 - behind
            was_sent(way, turn % PIECES, half if turn >= 0 else half - 1)
    send_back.wait_recv()
    out_ref[...] += arrived[...]
    send_back.wait_send()


def shards(sim_embed, real_embed):
    devices = lax.axis_size("blk")
    chips = devices // CORES
    half = chips // 2
    rows, width = sim_embed.shape
    rows_real = real_embed.shape[0]
    pairs = CORES * rows * (rows + rows_real) * chips
    return pl.pallas_call(
        functools.partial(kernel, chips, rows * devices, rows_real * devices),
        out_shape=jax.ShapeDtypeStruct((rows, width), jnp.float32),
        in_specs=[pl.BlockSpec(memory_space=pltpu.HBM)] * 2,
        out_specs=pl.BlockSpec(memory_space=pltpu.VMEM),
        scratch_shapes=[
            pltpu.VMEM((half, 2, rows, width), jnp.bfloat16),
            pltpu.VMEM((half, 2, rows_real, width), jnp.bfloat16),
            pltpu.VMEM((CORES, rows, width), jnp.bfloat16),
            pltpu.VMEM((rows_real, width), jnp.bfloat16),
            pltpu.VMEM((CORES * rows, width), jnp.float32),
            pltpu.VMEM((rows, width), jnp.float32),
            pltpu.VMEM((rows, width), jnp.float32),
            pltpu.SemaphoreType.DMA((2, PIECES, half)),
            pltpu.SemaphoreType.DMA((2, PIECES, half)),
            pltpu.SemaphoreType.DMA((2,)),
            pltpu.SemaphoreType.DMA((2,)),
            pltpu.SemaphoreType.DMA((2,)),
        ],
        compiler_params=pltpu.CompilerParams(
            collective_id=0, has_side_effects=True, vmem_limit_bytes=48 * 1024 * 1024
        ),
        cost_estimate=pl.CostEstimate(
            flops=4 * pairs * width, bytes_accessed=6 * rows * width, transcendentals=pairs
        ),
    )(*(pltpu.with_memory_space_constraint(x, pltpu.HBM) for x in (sim_embed, real_embed)))


def solution(mesh):
    in_specs = (P(("grp", "blk"), None), P(("grp", "blk"), None))
    out_specs = P(("grp", "blk"), None)
    return jax.shard_map(shards, mesh=mesh, in_specs=in_specs, out_specs=out_specs, check_vma=False)
```
